32 devices in a mesh: grp: 4 (over x, core), wide: 8 (over z, y).
Axes of the slice: x: 2, y: 2, z: 4, core: 2. Of those that a mesh axis runs over, the one named last changes fastest.
Arguments:
- velocity: float32 [3, 64, 128, 512], P(None, 'grp', 'wide'), may hold values from -6 to 6
- level_set: float32 [64, 128, 512], P('grp', 'wide'), may hold values from -8 to 8
Outputs:
- force: float32 [3, 64, 128, 512], P(None, 'grp', 'wide')
The draws below stay inside these ranges and needn't reach their ends.
All inputs are finite; a program needn't handle non-finite values.
Results may differ from the reference program's by a relative error of at most 0.000054.
Values sent between devices are 32-bit elements; how exact they have to be, the bound alone decides.
No kernel may reach another device: no remote copies, remote signals or barrier semaphores. Data moves between devices by JAX's collectives and lax.ppermute only.
A program may use at most 64 MiB of HBM per device.

```python
import jax
import jax.numpy as jnp
import numpy as np
from jax import lax

NX = 512
NY = 128
NZ = 64


def steps_of(rng, extent, pieces, low, top_value):
    level = 1.0
    for position, shards_of in pieces:
        steps = jax.random.uniform(jax.random.fold_in(jax.random.fold_in(rng, 6), position), (shards_of,), jnp.float32, low / len(pieces), top_value / len(pieces))
        level = level * jnp.repeat(jnp.exp(steps), extent[position] // shards_of).reshape((-1,) + (1,) * (len(extent) - 1 - position))
    return level


def bell_draw(stream_key, extent, scale, limit, pieces=(), held_as=jnp.bfloat16):
    array = scale * jax.random.normal(stream_key, extent, jnp.float32)
    if pieces:
        array = array * steps_of(stream_key, extent, pieces, -0.22, 0.18)
    return jnp.clip(array, -limit, limit).astype(held_as)


def setup_inputs(seed: int = 0) -> dict:
    seeds = jax.random.split(jax.random.key(seed), 3)
    velocity = bell_draw(seeds[0], (3, NZ, NY, NX), 1.0, 6.0, ((1, 4), (2, 8)), jnp.float32)
    level_set = bell_draw(seeds[1], (NZ, NY, NX), 1.5, 8.0, ((0, 4), (1, 8)), jnp.float32)
    return dict(velocity=velocity, level_set=level_set)


interface_width = 1.0


def derivative_table(count):
    offsets = np.arange(count)
    offset_mod = (offsets[:, None] - offsets[None, :]) % count
    angle_arg = np.pi * offset_mod / count
    safe_angle = np.where(offset_mod == 0, 0.5, angle_arg)
    parity = np.where(offset_mod % 2 == 0, 1.0, -1.0)
    entries = (np.pi / count) * parity * np.cos(safe_angle) / np.sin(safe_angle)
    return np.where(offset_mod == 0, 0.0, entries).astype(np.float32)


def along_last(source, table_t):
    return jnp.dot(source, table_t, precision=lax.Precision.HIGHEST)


def properties(level_set):
    heavy = 0.5 * (1.0 + jnp.tanh(level_set / interface_width))
    return 0.2 + 0.8 * heavy, 0.25 + 0.75 * heavy


def reference(velocity, level_set):
    dx_t = jnp.asarray(derivative_table(NX).T)
    dy_t = jnp.asarray(derivative_table(NY).T)
    dz_full = jnp.asarray(derivative_table(NZ))
    viscosity_all, unused_density = properties(level_set)
    dz_visc = jnp.dot(dz_full, viscosity_all.reshape(NZ, NY * NX), precision=lax.Precision.HIGHEST).reshape(NZ, NY, NX)

    def yderiv(source):
        return jnp.swapaxes(along_last(jnp.swapaxes(source, -1, -2), dy_t), -1, -2)

    def one_plane(inputs):
        vel_plane, level_plane, dz_plane = inputs
        viscosity, density = properties(level_plane)
        grad_x = along_last(vel_plane, dx_t)
        grad_y = yderiv(vel_plane)
        s_xx = 2.0 * viscosity * grad_x[0]
        s_xy = viscosity * (grad_y[0] + grad_x[1])
        s_yy = 2.0 * viscosity * grad_y[1]
        s_xz = viscosity * grad_x[2]
        s_yz = viscosity * grad_y[2]
        dx_stress = along_last(jnp.stack([s_xx, s_xy, s_xz]), dx_t)
        dy_stress = yderiv(jnp.stack([s_xy, s_yy, s_yz]))
        first = (dx_stress[0] + dy_stress[0] + dz_plane * grad_x[2]) / density
        second = (dx_stress[1] + dy_stress[1] + dz_plane * grad_y[2]) / density
        third = (dx_stress[2] + dy_stress[2]) / density
        return jnp.stack([first, second, third])

    planes = lax.map(one_plane, (jnp.moveaxis(velocity, 1, 0), level_set, dz_visc))
    return jnp.moveaxis(planes, 0, 1)
```

```python
import functools

import jax
import jax.numpy as jnp
import numpy as np
from jax import lax
from jax.experimental import pallas as pl
from jax.experimental.pallas import tpu as pltpu
from jax.sharding import PartitionSpec as P

interface_width = 1.0
vmem_bytes = 40 * 1024 * 1024


def derivative_table(count):
    offsets = np.arange(count)
    offset_mod = (offsets[:, None] - offsets[None, :]) % count
    angle_arg = np.pi * offset_mod / count
    safe_angle = np.where(offset_mod == 0, 0.5, angle_arg)
    parity = np.where(offset_mod % 2 == 0, 1.0, -1.0)
    entries = np.pi / count * parity * np.cos(safe_angle) / np.sin(safe_angle)
    return np.where(offset_mod == 0, 0.0, entries).astype(np.float32)


def halves(table):
    high = table.astype(jnp.bfloat16)
    low = (table - high.astype(np.float32)).astype(jnp.bfloat16)
    return high, low


def along_last(source, table_t):
    return jnp.dot(source, table_t, precision=lax.Precision.HIGHEST)


def properties(level_set):
    heavy = 0.5 * (1.0 + jnp.tanh(level_set / interface_width))
    return (0.2 + 0.8 * heavy, 0.25 + 0.75 * heavy)


def pack_kernel(count, planes, chunk, velocity, level_set, *refs):
    outs, sems = refs[:count], refs[count]
    me = lax.axis_index("wide")
    copies = []
    for step in range(count):
        plane = (me ^ step) * planes + chunk
        copies.append(
            pltpu.make_async_copy(velocity.at[:, plane], outs[step].at[0:3], sems.at[step, 0])
        )
        copies.append(
            pltpu.make_async_copy(level_set.at[plane], outs[step].at[3], sems.at[step, 1])
        )
    for copy in copies:
        copy.start()
    for copy in copies:
        copy.wait()


def pack(velocity, level_set, count, planes, chunk):
    rows, cells = level_set.shape[1:]
    piece = jax.ShapeDtypeStruct((4, rows, cells), jnp.float32)
    return pl.pallas_call(
        functools.partial(pack_kernel, count, planes, chunk),
        out_shape=(piece,) * count,
        in_specs=[pl.BlockSpec(memory_space=pl.ANY)] * 2,
        out_specs=(pl.BlockSpec(memory_space=pl.ANY),) * count,
        scratch_shapes=[pltpu.SemaphoreType.DMA((count, 2))],
        cost_estimate=pl.CostEstimate(
            flops=0, transcendentals=0, bytes_accessed=2 * count * 16 * rows * cells
        ),
        name="pack",
    )(velocity, level_set)


def split(value):
    high = value.astype(jnp.bfloat16)
    low = (value - high.astype(jnp.float32)).astype(jnp.bfloat16)
    return high, low


def times_x(fields, table):
    high, low = split(fields)
    return jnp.dot(
        jnp.concatenate([high, low, high], axis=1), table, preferred_element_type=jnp.float32
    )


def times_y(table, fields):
    high, low = split(fields)
    return jnp.dot(
        table, jnp.concatenate([high, high, low], axis=0), preferred_element_type=jnp.float32
    )


def plane_kernel(count, dx, dy, *refs):
    pieces, outs = refs[:count], refs[count : 2 * count]
    held, result = refs[2 * count :]
    me = lax.axis_index("wide")
    rows, cells = pieces[0].shape[1:]
    lines = rows * count
    for step in range(count):
        held[:, pl.ds(pl.multiple_of((me ^ step) * rows, 8), rows), :] = pieces[step][...]
    heavy = 0.5 * (1.0 + jnp.tanh(held[3] / interface_width))
    viscosity = 0.2 + 0.8 * heavy
    grad_x = times_x(held[0:3].reshape(3 * lines, cells), dx[...]).reshape(3, lines, cells)
    grad_y = times_y(dy[...], jnp.concatenate([held[0], held[1], held[2]], axis=1))
    grad_yu, grad_yv, grad_yw = (grad_y[:, i * cells : (i + 1) * cells] for i in range(3))
    s_xx = 2.0 * viscosity * grad_x[0]
    s_xy = viscosity * (grad_yu + grad_x[1])
    s_xz = viscosity * grad_x[2]
    s_yy = 2.0 * viscosity * grad_yv
    s_yz = viscosity * grad_yw
    along_x = times_x(jnp.concatenate([s_xx, s_xy, s_xz], axis=0), dx[...])
    along_y = times_y(dy[...], jnp.concatenate([s_xy, s_yy, s_yz], axis=1))
    for i in range(3):
        result[i] = (
            along_x[i * lines : (i + 1) * lines] + along_y[:, i * cells : (i + 1) * cells]
        )
    result[3] = grad_yw
    for step in range(count):
        outs[step][...] = result[:, pl.ds(pl.multiple_of((me ^ step) * rows, 8), rows), :]


def on_plane(pieces, dx, dy):
    count = len(pieces)
    rows, cells = pieces[0].shape[1:]
    lines = rows * count
    piece = jax.ShapeDtypeStruct((4, rows, cells), jnp.float32)
    vmem = pl.BlockSpec(memory_space=pltpu.VMEM)
    return pl.pallas_call(
        functools.partial(plane_kernel, count),
        out_shape=(piece,) * count,
        in_specs=[vmem] * (2 + count),
        out_specs=(vmem,) * count,
        scratch_shapes=[pltpu.VMEM((4, lines, cells), jnp.float32)] * 2,
        compiler_params=pltpu.CompilerParams(vmem_limit_bytes=vmem_bytes),
        cost_estimate=pl.CostEstimate(
            flops=36 * lines * cells * (cells + lines),
            transcendentals=lines * cells,
            bytes_accessed=32 * lines * cells,
        ),
        name="plane",
    )(dx, dy, *pieces)


def join_kernel(count, planes, *refs):
    pieces = refs[: count * planes]
    inverse, first_add, cross, out = refs[count * planes :]
    me = lax.axis_index("wide")
    for step in range(count):
        for chunk in range(planes):
            plane = (me ^ step) * planes + chunk
            piece = pieces[chunk * count + step]
            scale = inverse[plane]
            out[0, plane] = piece[0] * scale + first_add[plane]
            out[1, plane] = piece[1] * scale + piece[3] * cross[plane]
            out[2, plane] = piece[2] * scale


def join(pieces, inverse, first_add, cross, count, planes):
    vmem = pl.BlockSpec(memory_space=pltpu.VMEM)
    return pl.pallas_call(
        functools.partial(join_kernel, count, planes),
        out_shape=jax.ShapeDtypeStruct((3,) + inverse.shape, jnp.float32),
        in_specs=[vmem] * (count * planes + 3),
        out_specs=vmem,
        compiler_params=pltpu.CompilerParams(vmem_limit_bytes=vmem_bytes),
        name="join",
    )(*pieces, inverse, first_add, cross)


def exchange(pieces, order):
    count = len(pieces)
    got = [pieces[0]] + [None] * (count - 1)
    for step in order:
        got[step] = lax.ppermute(pieces[step], "wide", [(i, i ^ step) for i in range(count)])
    return got


def by_planes(velocity, level_set):
    cells_x = velocity.shape[3]
    slab_z, slab_y = velocity.shape[1:3]
    count = lax.axis_size("wide")
    group_count = lax.axis_size("grp")
    planes = slab_z // count
    table_x = derivative_table(cells_x).T
    high, low = halves(table_x)
    dx = jnp.asarray(np.concatenate([high, high, low], axis=0))
    high, low = halves(derivative_table(slab_y * count))
    dy = jnp.asarray(np.concatenate([high, low, high], axis=1))
    far = list(range(count // 2, count))
    near = list(range(1, count // 2))
    order = [step for pair in zip(far, near + [None]) for step in pair if step is not None]

    arrived = [
        exchange(pack(velocity, level_set, count, planes, chunk), order) for chunk in range(planes)
    ]
    returned = []
    for chunk in range(planes):
        returned += exchange(on_plane(arrived[chunk], dx, dy), order)

    viscosity, density = properties(level_set)
    whole = lax.all_gather(viscosity, "grp", axis=0, tiled=True)
    dz_rows = lax.dynamic_slice_in_dim(
        jnp.asarray(derivative_table(slab_z * group_count)),
        lax.axis_index("grp") * slab_z,
        slab_z,
        0,
    )
    dz_visc = jnp.einsum("ij,jyx->iyx", dz_rows, whole, precision=lax.Precision.HIGHEST)
    inverse = 1.0 / density
    cross = dz_visc * inverse
    first_add = cross * along_last(velocity[2], jnp.asarray(table_x))
    return join(returned, inverse, first_add, cross, count, planes)


def by_lines(velocity, level_set):
    cells_x = velocity.shape[3]
    slab_z = velocity.shape[1]
    slab_y = velocity.shape[2]
    wide_count = lax.axis_size("wide")
    group_count = lax.axis_size("grp")
    cells_y = slab_y * wide_count
    cells_z = slab_z * group_count
    dx_t = jnp.asarray(derivative_table(cells_x).T)
    dy_full = jnp.asarray(derivative_table(cells_y))
    dz_full = jnp.asarray(derivative_table(cells_z))
    viscosity, density = properties(level_set)
    z_columns = slab_y * cells_x // group_count
    y_columns = slab_z * cells_x // wide_count
    visc_panels = viscosity.reshape(slab_z, group_count, z_columns)
    result = jnp.einsum(
        "ij,jgk->igk",
        dz_full,
        lax.all_to_all(visc_panels, "grp", split_axis=1, concat_axis=0, tiled=True),
        precision=lax.Precision.HIGHEST,
    )
    dz_visc = lax.all_to_all(result, "grp", split_axis=0, concat_axis=1, tiled=True).reshape(
        slab_z, slab_y, cells_x
    )

    def to_lines(field):
        count = field.shape[0]
        return jnp.transpose(field, (0, 2, 1, 3)).reshape(count, slab_y, wide_count, y_columns)

    def from_lines(field):
        count = field.shape[0]
        return jnp.transpose(field.reshape(count, slab_y, slab_z, cells_x), (0, 2, 1, 3))

    def yline(block):
        return jnp.einsum("ij,cjgk->cigk", dy_full, block, precision=lax.Precision.HIGHEST)

    def y_derivative(field):
        lines = lax.all_to_all(to_lines(field), "wide", split_axis=2, concat_axis=1, tiled=True)
        return from_lines(
            lax.all_to_all(yline(lines), "wide", split_axis=1, concat_axis=2, tiled=True)
        )

    grad_x = along_last(velocity, dx_t)
    grad_y = y_derivative(velocity)
    s_xx = 2.0 * viscosity * grad_x[0]
    s_xy = viscosity * (grad_y[0] + grad_x[1])
    s_yy = 2.0 * viscosity * grad_y[1]
    s_xz = viscosity * grad_x[2]
    s_yz = viscosity * grad_y[2]
    dy_stress = y_derivative(jnp.stack([s_xy, s_yy, s_yz]))
    dx_stress = along_last(jnp.stack([s_xx, s_xy, s_xz]), dx_t)
    first = (dx_stress[0] + dy_stress[0] + dz_visc * grad_x[2]) / density
    second = (dx_stress[1] + dy_stress[1] + dz_visc * grad_y[2]) / density
    third = (dx_stress[2] + dy_stress[2]) / density
    return jnp.stack([first, second, third])


def shards(velocity, level_set):
    count = lax.axis_size("wide")
    if count & (count - 1) == 0 and velocity.shape[1] % count == 0:
        return by_planes(velocity, level_set)
    return by_lines(velocity, level_set)


def solution(mesh):
    return jax.shard_map(
        shards,
        mesh=mesh,
        in_specs=(P(None, "grp", "wide", None), P("grp", "wide", None)),
        out_specs=P(None, "grp", "wide", None),
        check_vma=False,
    )
```

```python
import functools

import jax
import jax.numpy as jnp
import numpy as np
from jax import lax
from jax.experimental import pallas as pl
from jax.experimental.pallas import tpu as pltpu
from jax.sharding import PartitionSpec as P

interface_width = 1.0
vmem_bytes = 40 * 1024 * 1024


def derivative_table(count):
    offsets = np.arange(count)
    offset_mod = (offsets[:, None] - offsets[None, :]) % count
    angle_arg = np.pi * offset_mod / count
    safe_angle = np.where(offset_mod == 0, 0.5, angle_arg)
    parity = np.where(offset_mod % 2 == 0, 1.0, -1.0)
    entries = np.pi / count * parity * np.cos(safe_angle) / np.sin(safe_angle)
    return np.where(offset_mod == 0, 0.0, entries).astype(np.float32)


def halves(table):
    high = table.astype(jnp.bfloat16)
    low = (table - high.astype(np.float32)).astype(jnp.bfloat16)
    return high, low


def along_last(source, table_t):
    return jnp.dot(source, table_t, precision=lax.Precision.HIGHEST)


def properties(level_set):
    heavy = 0.5 * (1.0 + jnp.tanh(level_set / interface_width))
    return (0.2 + 0.8 * heavy, 0.25 + 0.75 * heavy)


def pack_kernel(count, planes, velocity, level_set, *outs):
    me = lax.axis_index("wide")
    for chunk in range(planes):
        for step in range(count):
            plane = (me ^ step) * planes + chunk
            outs[chunk * count + step][0:3] = velocity[:, plane]
            outs[chunk * count + step][3] = level_set[plane]


def pack(velocity, level_set, count, planes):
    rows, cells = level_set.shape[1:]
    piece = jax.ShapeDtypeStruct((4, rows, cells), jnp.float32)
    vmem = pl.BlockSpec(memory_space=pltpu.VMEM)
    return pl.pallas_call(
        functools.partial(pack_kernel, count, planes),
        out_shape=(piece,) * (count * planes),
        in_specs=[vmem] * 2,
        out_specs=(vmem,) * (count * planes),
        compiler_params=pltpu.CompilerParams(vmem_limit_bytes=vmem_bytes),
        cost_estimate=pl.CostEstimate(
            flops=0, transcendentals=0, bytes_accessed=2 * count * planes * 16 * rows * cells
        ),
        name="pack",
    )(velocity, level_set)


def split(value):
    high = value.astype(jnp.bfloat16)
    low = (value - high.astype(jnp.float32)).astype(jnp.bfloat16)
    return high, low


def times_x(fields, table):
    high, low = split(fields)
    return jnp.dot(
        jnp.concatenate([high, low, high], axis=1), table, preferred_element_type=jnp.float32
    )


def times_y(table, fields):
    high, low = split(fields)
    return jnp.dot(
        table, jnp.concatenate([high, high, low], axis=0), preferred_element_type=jnp.float32
    )


def plane_kernel(count, dx, dy, *refs):
    pieces, outs = refs[:count], refs[count : 2 * count]
    held, result = refs[2 * count :]
    me = lax.axis_index("wide")
    rows, cells = pieces[0].shape[1:]
    lines = rows * count
    for step in range(count):
        held[:, pl.ds(pl.multiple_of((me ^ step) * rows, 8), rows), :] = pieces[step][...]
    heavy = 0.5 * (1.0 + jnp.tanh(held[3] / interface_width))
    viscosity = 0.2 + 0.8 * heavy
    grad_x = times_x(held[0:3].reshape(3 * lines, cells), dx[...]).reshape(3, lines, cells)
    grad_y = times_y(dy[...], jnp.concatenate([held[0], held[1], held[2]], axis=1))
    grad_yu, grad_yv, grad_yw = (grad_y[:, i * cells : (i + 1) * cells] for i in range(3))
    s_xx = 2.0 * viscosity * grad_x[0]
    s_xy = viscosity * (grad_yu + grad_x[1])
    s_xz = viscosity * grad_x[2]
    s_yy = 2.0 * viscosity * grad_yv
    s_yz = viscosity * grad_yw
    along_x = times_x(jnp.concatenate([s_xx, s_xy, s_xz], axis=0), dx[...])
    along_y = times_y(dy[...], jnp.concatenate([s_xy, s_yy, s_yz], axis=1))
    for i in range(3):
        result[i] = (
            along_x[i * lines : (i + 1) * lines] + along_y[:, i * cells : (i + 1) * cells]
        )
    result[3] = grad_yw
    for step in range(count):
        outs[step][...] = result[:, pl.ds(pl.multiple_of((me ^ step) * rows, 8), rows), :]


def on_plane(pieces, dx, dy):
    count = len(pieces)
    rows, cells = pieces[0].shape[1:]
    lines = rows * count
    piece = jax.ShapeDtypeStruct((4, rows, cells), jnp.float32)
    vmem = pl.BlockSpec(memory_space=pltpu.VMEM)
    return pl.pallas_call(
        functools.partial(plane_kernel, count),
        out_shape=(piece,) * count,
        in_specs=[vmem] * (2 + count),
        out_specs=(vmem,) * count,
        scratch_shapes=[pltpu.VMEM((4, lines, cells), jnp.float32)] * 2,
        compiler_params=pltpu.CompilerParams(vmem_limit_bytes=vmem_bytes),
        cost_estimate=pl.CostEstimate(
            flops=36 * lines * cells * (cells + lines),
            transcendentals=lines * cells,
            bytes_accessed=32 * lines * cells,
        ),
        name="plane",
    )(dx, dy, *pieces)


def join_kernel(count, planes, *refs):
    pieces = refs[: count * planes]
    inverse, first_add, cross, out = refs[count * planes :]
    me = lax.axis_index("wide")
    for step in range(count):
        for chunk in range(planes):
            plane = (me ^ step) * planes + chunk
            piece = pieces[chunk * count + step]
            scale = inverse[plane]
            out[0, plane] = piece[0] * scale + first_add[plane]
            out[1, plane] = piece[1] * scale + piece[3] * cross[plane]
            out[2, plane] = piece[2] * scale


def join(pieces, inverse, first_add, cross, count, planes):
    vmem = pl.BlockSpec(memory_space=pltpu.VMEM)
    return pl.pallas_call(
        functools.partial(join_kernel, count, planes),
        out_shape=jax.ShapeDtypeStruct((3,) + inverse.shape, jnp.float32),
        in_specs=[vmem] * (count * planes + 3),
        out_specs=vmem,
        compiler_params=pltpu.CompilerParams(vmem_limit_bytes=vmem_bytes),
        name="join",
    )(*pieces, inverse, first_add, cross)


def exchange(pieces, order):
    count = len(pieces)
    got = [pieces[0]] + [None] * (count - 1)
    for step in order:
        got[step] = lax.ppermute(pieces[step], "wide", [(i, i ^ step) for i in range(count)])
    return got


def by_planes(velocity, level_set):
    cells_x = velocity.shape[3]
    slab_z, slab_y = velocity.shape[1:3]
    count = lax.axis_size("wide")
    group_count = lax.axis_size("grp")
    planes = slab_z // count
    table_x = derivative_table(cells_x).T
    high, low = halves(table_x)
    dx = jnp.asarray(np.concatenate([high, high, low], axis=0))
    high, low = halves(derivative_table(slab_y * count))
    dy = jnp.asarray(np.concatenate([high, low, high], axis=1))
    far = list(range(count // 2, count))
    near = list(range(1, count // 2))
    order = [step for pair in zip(far, near + [None]) for step in pair if step is not None]

    pieces = pack(velocity, level_set, count, planes)
    arrived = [exchange(pieces[i * count : (i + 1) * count], order) for i in range(planes)]
    returned = []
    for chunk in range(planes):
        returned += exchange(on_plane(arrived[chunk], dx, dy), order)

    viscosity, density = properties(level_set)
    dz_full = derivative_table(slab_z * group_count)
    dz_blocks = jnp.asarray(dz_full.reshape(group_count, slab_z, group_count, slab_z))
    place = lax.axis_index("grp")
    dz_visc = 0.0
    for turn in range(group_count):
        slab = viscosity
        if turn:
            slab = lax.ppermute(
                viscosity, "grp", [(i, (i + turn) % group_count) for i in range(group_count)]
            )
        owner = lax.rem(place - turn + group_count, group_count)
        dz_visc += jnp.einsum(
            "ij,jyx->iyx", dz_blocks[place, :, owner], slab, precision=lax.Precision.HIGHEST
        )
    inverse = 1.0 / density
    cross = dz_visc * inverse
    first_add = cross * along_last(velocity[2], jnp.asarray(table_x))
    return join(returned, inverse, first_add, cross, count, planes)


def by_lines(velocity, level_set):
    cells_x = velocity.shape[3]
    slab_z = velocity.shape[1]
    slab_y = velocity.shape[2]
    wide_count = lax.axis_size("wide")
    group_count = lax.axis_size("grp")
    cells_y = slab_y * wide_count
    cells_z = slab_z * group_count
    dx_t = jnp.asarray(derivative_table(cells_x).T)
    dy_full = jnp.asarray(derivative_table(cells_y))
    dz_full = jnp.asarray(derivative_table(cells_z))
    viscosity, density = properties(level_set)
    z_columns = slab_y * cells_x // group_count
    y_columns = slab_z * cells_x // wide_count
    visc_panels = viscosity.reshape(slab_z, group_count, z_columns)
    result = jnp.einsum(
        "ij,jgk->igk",
        dz_full,
        lax.all_to_all(visc_panels, "grp", split_axis=1, concat_axis=0, tiled=True),
        precision=lax.Precision.HIGHEST,
    )
    dz_visc = lax.all_to_all(result, "grp", split_axis=0, concat_axis=1, tiled=True).reshape(
        slab_z, slab_y, cells_x
    )

    def to_lines(field):
        count = field.shape[0]
        return jnp.transpose(field, (0, 2, 1, 3)).reshape(count, slab_y, wide_count, y_columns)

    def from_lines(field):
        count = field.shape[0]
        return jnp.transpose(field.reshape(count, slab_y, slab_z, cells_x), (0, 2, 1, 3))

    def yline(block):
        return jnp.einsum("ij,cjgk->cigk", dy_full, block, precision=lax.Precision.HIGHEST)

    def y_derivative(field):
        lines = lax.all_to_all(to_lines(field), "wide", split_axis=2, concat_axis=1, tiled=True)
        return from_lines(
            lax.all_to_all(yline(lines), "wide", split_axis=1, concat_axis=2, tiled=True)
        )

    grad_x = along_last(velocity, dx_t)
    grad_y = y_derivative(velocity)
    s_xx = 2.0 * viscosity * grad_x[0]
    s_xy = viscosity * (grad_y[0] + grad_x[1])
    s_yy = 2.0 * viscosity * grad_y[1]
    s_xz = viscosity * grad_x[2]
    s_yz = viscosity * grad_y[2]
    dy_stress = y_derivative(jnp.stack([s_xy, s_yy, s_yz]))
    dx_stress = along_last(jnp.stack([s_xx, s_xy, s_xz]), dx_t)
    first = (dx_stress[0] + dy_stress[0] + dz_visc * grad_x[2]) / density
    second = (dx_stress[1] + dy_stress[1] + dz_visc * grad_y[2]) / density
    third = (dx_stress[2] + dy_stress[2]) / density
    return jnp.stack([first, second, third])


def shards(velocity, level_set):
    count = lax.axis_size("wide")
    if count & (count - 1) == 0 and velocity.shape[1] % count == 0:
        return by_planes(velocity, level_set)
    return by_lines(velocity, level_set)


def solution(mesh):
    return jax.shard_map(
        shards,
        mesh=mesh,
        in_specs=(P(None, "grp", "wide", None), P("grp", "wide", None)),
        out_specs=P(None, "grp", "wide", None),
        check_vma=False,
    )
```

```python
import functools

import jax
import jax.numpy as jnp
import numpy as np
from jax import lax
from jax.experimental import pallas as pl
from jax.experimental.pallas import tpu as pltpu
from jax.sharding import PartitionSpec as P

interface_width = 1.0
flight = 5
mebibyte = 1024 * 1024
no_cost = pl.CostEstimate(flops=0, transcendentals=0, bytes_accessed=0)
small_cost = pl.CostEstimate(flops=10_000_000, transcendentals=0, bytes_accessed=0)


def derivative_table(count):
    offsets = np.arange(count)
    offset_mod = (offsets[:, None] - offsets[None, :]) % count
    angle_arg = np.pi * offset_mod / count
    safe_angle = np.where(offset_mod == 0, 0.5, angle_arg)
    parity = np.where(offset_mod % 2 == 0, 1.0, -1.0)
    entries = np.pi / count * parity * np.cos(safe_angle) / np.sin(safe_angle)
    return np.where(offset_mod == 0, 0.0, entries).astype(np.float32)


def halves(table):
    high = table.astype(jnp.bfloat16)
    low = (table - high.astype(np.float32)).astype(jnp.bfloat16)
    return high, low


def along_last(source, table_t):
    return jnp.dot(source, table_t, precision=lax.Precision.HIGHEST)


def properties(level_set):
    heavy = 0.5 * (1.0 + jnp.tanh(level_set / interface_width))
    return (0.2 + 0.8 * heavy, 0.25 + 0.75 * heavy)


def pack_kernel(steps, planes, velocity, level_set, *refs):
    outs, sems = refs[-1 - len(steps) : -1], refs[-1]
    me = lax.axis_index("wide")
    copies = []
    for i, (out, (chunk, step)) in enumerate(zip(outs, steps)):
        plane = (me ^ step) * planes + chunk
        copies += [
            pltpu.make_async_copy(velocity.at[:, plane], out.at[0:3], sems.at[i, 0]),
            pltpu.make_async_copy(level_set.at[plane], out.at[3], sems.at[i, 1]),
        ]
    for copy in copies:
        copy.start()
    for copy in copies:
        copy.wait()


def pack(velocity, level_set, steps, planes, after=()):
    rows, cells = level_set.shape[1:]
    whole = pl.BlockSpec(memory_space=pl.ANY)
    hbm = pl.BlockSpec(memory_space=pltpu.HBM)
    return pl.pallas_call(
        functools.partial(pack_kernel, steps, planes),
        out_shape=(jax.ShapeDtypeStruct((4, rows, cells), jnp.float32),) * len(steps),
        in_specs=[hbm] * 2 + [whole] * len(after),
        out_specs=(pl.BlockSpec(memory_space=pltpu.VMEM),) * len(steps),
        scratch_shapes=[pltpu.SemaphoreType.DMA((len(steps), 2))],
        compiler_params=pltpu.CompilerParams(vmem_limit_bytes=(4 if after else 61) * mebibyte),
        cost_estimate=no_cost,
        name="pack",
    )(velocity, level_set, *after)


def split(value):
    high = value.astype(jnp.bfloat16)
    low = (value - high.astype(jnp.float32)).astype(jnp.bfloat16)
    return high, low


def times_x(fields, table):
    high, low = split(fields)
    return jnp.dot(
        jnp.concatenate([high, low, high], axis=1), table, preferred_element_type=jnp.float32
    )


def times_y(table, fields):
    high, low = split(fields)
    return jnp.dot(
        table, jnp.concatenate([high, high, low], axis=0), preferred_element_type=jnp.float32
    )


def plane_kernel(count, dx, dy, *refs):
    pieces, outs = refs[:count], refs[count : 2 * count]
    held, result = refs[2 * count :]
    me = lax.axis_index("wide")
    rows, cells = pieces[0].shape[1:]
    lines = rows * count
    for step in range(count):
        held[:, pl.ds(pl.multiple_of((me ^ step) * rows, 8), rows), :] = pieces[step][...]
    heavy = 0.5 * (1.0 + jnp.tanh(held[3] / interface_width))
    viscosity = 0.2 + 0.8 * heavy
    grad_x = times_x(held[0:3].reshape(3 * lines, cells), dx[...]).reshape(3, lines, cells)
    grad_y = times_y(dy[...], jnp.concatenate([held[0], held[1], held[2]], axis=1))
    grad_yu, grad_yv, grad_yw = (grad_y[:, i * cells : (i + 1) * cells] for i in range(3))
    s_xx = 2.0 * viscosity * grad_x[0]
    s_xy = viscosity * (grad_yu + grad_x[1])
    s_xz = viscosity * grad_x[2]
    s_yy = 2.0 * viscosity * grad_yv
    s_yz = viscosity * grad_yw
    along_x = times_x(jnp.concatenate([s_xx, s_xy, s_xz], axis=0), dx[...])
    along_y = times_y(dy[...], jnp.concatenate([s_xy, s_yy, s_yz], axis=1))
    for i in range(3):
        result[i] = (
            along_x[i * lines : (i + 1) * lines] + along_y[:, i * cells : (i + 1) * cells]
        )
    result[3] = grad_yw
    for step in range(count):
        outs[step][...] = result[:, pl.ds(pl.multiple_of((me ^ step) * rows, 8), rows), :]


def on_plane(pieces, dx, dy):
    count = len(pieces)
    rows, cells = pieces[0].shape[1:]
    vmem = pl.BlockSpec(memory_space=pltpu.VMEM)
    return pl.pallas_call(
        functools.partial(plane_kernel, count),
        out_shape=(jax.ShapeDtypeStruct((4, rows, cells), jnp.float32),) * count,
        in_specs=[vmem] * (2 + count),
        out_specs=(vmem,) * count,
        scratch_shapes=[pltpu.VMEM((4, rows * count, cells), jnp.float32)] * 2,
        compiler_params=pltpu.CompilerParams(vmem_limit_bytes=16 * mebibyte),
        cost_estimate=no_cost,
        name="plane",
    )(dx, dy, *pieces)


def join_kernel(steps, planes, *refs):
    pieces = refs[: len(steps)]
    inverse, first_add, cross = refs[len(steps) : len(steps) + 3]
    out, held, sems = refs[-3:]
    me = lax.axis_index("wide")
    copies = []
    for i, (chunk, step) in enumerate(steps):
        plane = (me ^ step) * planes + chunk
        piece = pieces[i]
        scale = inverse[plane]
        held[i, 0] = piece[0] * scale + first_add[plane]
        held[i, 1] = piece[1] * scale + piece[3] * cross[plane]
        held[i, 2] = piece[2] * scale
        copies.append(pltpu.make_async_copy(held.at[i], out.at[:, plane], sems.at[i]))
        copies[-1].start()
    for copy in copies:
        copy.wait()


def join(steps, pieces, fields, planes, total=None):
    shape = fields[0].shape
    vmem = pl.BlockSpec(memory_space=pltpu.VMEM)
    whole = pl.BlockSpec(memory_space=pl.ANY)
    extra = [] if total is None else [total]
    return pl.pallas_call(
        functools.partial(join_kernel, steps, planes),
        out_shape=jax.ShapeDtypeStruct((3,) + shape, jnp.float32),
        in_specs=[vmem] * (len(steps) + 3) + [whole] * len(extra),
        out_specs=whole,
        input_output_aliases={len(steps) + 3: 0} if extra else {},
        scratch_shapes=[
            pltpu.VMEM((len(steps), 3) + shape[1:], jnp.float32),
            pltpu.SemaphoreType.DMA((len(steps),)),
        ],
        compiler_params=pltpu.CompilerParams(vmem_limit_bytes=8 * mebibyte),
        cost_estimate=small_cost,
        name="join",
    )(*pieces, *fields, *extra)


def panel_kernel(count, level_set, after, *refs):
    outs, (held, sem) = refs[:count], refs[count:]
    copy = pltpu.make_async_copy(level_set, held, sem)
    copy.start()
    copy.wait()
    heavy = 0.5 * (1.0 + jnp.tanh(held[...] / interface_width))
    held[...] = 0.2 + 0.8 * heavy
    me = lax.axis_index("grp")
    width = outs[0].shape[2]
    for step in range(count):
        outs[step][...] = held[:, :, pl.ds(pl.multiple_of((me ^ step) * width, 128), width)]


def panels(level_set, after, count):
    slab, rows, cells = level_set.shape
    vmem = pl.BlockSpec(memory_space=pltpu.VMEM)
    return pl.pallas_call(
        functools.partial(panel_kernel, count),
        out_shape=(jax.ShapeDtypeStruct((slab, rows, cells // count), jnp.float32),) * count,
        in_specs=[pl.BlockSpec(memory_space=pltpu.HBM), pl.BlockSpec(memory_space=pl.ANY)],
        out_specs=(vmem,) * count,
        scratch_shapes=[pltpu.VMEM((slab, rows, cells), jnp.float32), pltpu.SemaphoreType.DMA],
        compiler_params=pltpu.CompilerParams(vmem_limit_bytes=6 * mebibyte),
        cost_estimate=no_cost,
        name="panels",
    )(level_set, after)


def z_lines_kernel(count, tables, *refs):
    parts, outs, held = refs[:count], refs[count : 2 * count], refs[-1]
    slab, rows, _ = parts[0].shape
    for step in range(count):
        held[step * slab : (step + 1) * slab] = parts[step][...]
    table = tables[lax.axis_index("grp")]
    for row in range(rows):
        line = jnp.dot(
            table,
            held[:, row, :],
            precision=lax.Precision.HIGHEST,
            preferred_element_type=jnp.float32,
        )
        for step in range(count):
            outs[step][:, row, :] = line[step * slab : (step + 1) * slab]


def z_lines(tables, parts):
    count = len(parts)
    slab, rows, width = parts[0].shape
    vmem = pl.BlockSpec(memory_space=pltpu.VMEM)
    return pl.pallas_call(
        functools.partial(z_lines_kernel, count),
        out_shape=(jax.ShapeDtypeStruct(parts[0].shape, jnp.float32),) * count,
        in_specs=[vmem] * (1 + count),
        out_specs=(vmem,) * count,
        scratch_shapes=[pltpu.VMEM((slab * count, rows, width), jnp.float32)],
        compiler_params=pltpu.CompilerParams(vmem_limit_bytes=6 * mebibyte),
        cost_estimate=no_cost,
        name="z_lines",
    )(tables, *parts)


def prepare_kernel(count, dx, level_set, velocity, *refs):
    parts, (inverse, first_add, cross) = refs[:count], refs[count : count + 3]
    held, sems = refs[count + 3 :]
    copies = [
        pltpu.make_async_copy(level_set, held.at[0], sems.at[0]),
        pltpu.make_async_copy(velocity.at[2], held.at[1], sems.at[1]),
    ]
    for copy in copies:
        copy.start()
    for copy in copies:
        copy.wait()
    me = lax.axis_index("grp")
    width = parts[0].shape[2]
    slab, rows, cells = level_set.shape
    heavy = 0.5 * (1.0 + jnp.tanh(held[0] / interface_width))
    inverse[...] = 1.0 / (0.25 + 0.75 * heavy)
    for step in range(count):
        here = pl.ds(pl.multiple_of((me ^ step) * width, 128), width)
        cross[:, :, here] = parts[step][...] * inverse[:, :, here]
    grad = times_x(held[1].reshape(slab * rows, cells), dx[...]).reshape(slab, rows, cells)
    first_add[...] = cross[...] * grad


def prepare(dx, level_set, velocity, parts):
    vmem = pl.BlockSpec(memory_space=pltpu.VMEM)
    whole = pl.BlockSpec(memory_space=pltpu.HBM)
    return pl.pallas_call(
        functools.partial(prepare_kernel, len(parts)),
        out_shape=(jax.ShapeDtypeStruct(level_set.shape, jnp.float32),) * 3,
        in_specs=[vmem, whole, whole] + [vmem] * len(parts),
        out_specs=(vmem,) * 3,
        scratch_shapes=[
            pltpu.VMEM((2,) + level_set.shape, jnp.float32),
            pltpu.SemaphoreType.DMA((2,)),
        ],
        compiler_params=pltpu.CompilerParams(vmem_limit_bytes=16 * mebibyte),
        cost_estimate=no_cost,
        name="prepare",
    )(dx, level_set, velocity, *parts)


def gate_kernel(*refs):
    pass


def gate(pieces, token, after):
    arrays = [*pieces, token]
    whole = pl.BlockSpec(memory_space=pl.ANY)
    outs = pl.pallas_call(
        gate_kernel,
        out_shape=tuple(jax.ShapeDtypeStruct(x.shape, x.dtype) for x in arrays),
        in_specs=[whole] * (len(arrays) + len(after)),
        out_specs=(whole,) * len(arrays),
        input_output_aliases={i: i for i in range(len(arrays))},
        compiler_params=pltpu.CompilerParams(vmem_limit_bytes=mebibyte),
        cost_estimate=small_cost,
        name="gate",
    )(*arrays, *after)
    return outs[:-1], outs[-1]


class Line:
    def __init__(self):
        self.arrived = []
        self.token = jnp.zeros((8, 128), jnp.float32)

    def send(self, piece, axis, step):
        count = lax.axis_size(axis)
        if len(self.arrived) >= flight:
            (piece,), self.token = gate([piece], self.token, [self.arrived[-flight]])
        got = lax.ppermute(piece, axis, [(i, i ^ step) for i in range(count)])
        self.arrived.append(got)
        return got


def turns(first, second):
    both = [x for pair in zip(first, second) for x in pair]
    shorter = min(len(first), len(second))
    return both + list(first[shorter:]) + list(second[shorter:])


def message_order(count, planes, group_count):
    far, near = range(count // 2, count), range(1, count // 2)
    out = [("out", chunk, step) for chunk in range(planes) for step in turns(far, near)]
    back = [("back", chunk, step) for chunk in range(planes - 1) for step in turns(far, near)]
    back += [("back", planes - 1, step) for step in turns(near, far)]
    first_z = count - 1
    second_z = max(len(out) + 3, first_z + 2 * (group_count - 2) + 1)
    order = []
    for place, message in enumerate(out + back + [None] * 2 * (second_z + 2 * group_count)):
        for start, kind in ((first_z, "z_out"), (second_z, "z_back")):
            step, odd = divmod(place - start, 2)
            if not odd and 0 <= step < group_count - 1:
                order.append((kind, 0, step + 1))
        if message is not None:
            order.append(message)
    return order


def by_planes(velocity, level_set):
    cells_x = velocity.shape[3]
    slab_z, slab_y = velocity.shape[1:3]
    count = lax.axis_size("wide")
    group_count = lax.axis_size("grp")
    planes = slab_z // count
    high, low = halves(derivative_table(cells_x).T)
    dx = jnp.asarray(np.concatenate([high, high, low], axis=0))
    high, low = halves(derivative_table(slab_y * count))
    dy = jnp.asarray(np.concatenate([high, low, high], axis=1))
    table_z = derivative_table(slab_z * group_count)
    table_z = table_z.reshape(group_count, slab_z, group_count, slab_z)
    partners = [place ^ np.arange(group_count) for place in range(group_count)]
    tables = jnp.asarray(
        np.stack([table_z[p][:, :, p].reshape((slab_z * group_count,) * 2) for p in partners])
    )

    order = message_order(count, planes, group_count)
    first = [(0, step) for kind, chunk, step in order if kind == "out" and chunk == 0]
    first = [piece for piece in first if piece[1] >= count // 2][:2]
    rest = [(c, step) for c in range(planes) for step in range(count) if (c, step) not in first]
    sent = dict(zip(first, pack(velocity, level_set, first, planes)))
    sent.update(zip(rest, pack(velocity, level_set, rest, planes, [sent[p] for p in first])))

    line = Line()
    arrived = {(c, 0): sent[c, 0] for c in range(planes)}
    result, returned = {}, {}
    panel, z_arrived, z_result, z_returned = None, {}, None, {}
    for kind, chunk, step in order:
        if kind == "out":
            arrived[chunk, step] = line.send(sent[chunk, step], "wide", step)
        elif kind == "back":
            if chunk not in result:
                result[chunk] = on_plane([arrived[chunk, i] for i in range(count)], dx, dy)
                returned[chunk, 0] = result[chunk][0]
            returned[chunk, step] = line.send(result[chunk][step], "wide", step)
        elif kind == "z_out":
            if panel is None:
                panel = panels(level_set, line.arrived[0], group_count)
                z_arrived[0] = panel[0]
            z_arrived[step] = line.send(panel[step], "grp", step)
        else:
            if z_result is None:
                z_result = z_lines(tables, [z_arrived[i] for i in range(group_count)])
                z_returned[0] = z_result[0]
            z_returned[step] = line.send(z_result[step], "grp", step)

    fields = prepare(dx, level_set, velocity, [z_returned[i] for i in range(group_count)])
    total = None
    early = [(c, i) for c in range(planes - 1) for i in range(count)] + [(planes - 1, 0)]
    late = [(c, step) for kind, c, step in order if kind == "back" and c == planes - 1]
    for steps in [early] + [[piece] for piece in late]:
        total = join(steps, [returned[piece] for piece in steps], fields, planes, total)
    return total


def by_lines(velocity, level_set):
    cells_x = velocity.shape[3]
    slab_z = velocity.shape[1]
    slab_y = velocity.shape[2]
    wide_count = lax.axis_size("wide")
    group_count = lax.axis_size("grp")
    cells_y = slab_y * wide_count
    cells_z = slab_z * group_count
    dx_t = jnp.asarray(derivative_table(cells_x).T)
    dy_full = jnp.asarray(derivative_table(cells_y))
    dz_full = jnp.asarray(derivative_table(cells_z))
    viscosity, density = properties(level_set)
    z_columns = slab_y * cells_x // group_count
    y_columns = slab_z * cells_x // wide_count
    visc_panels = viscosity.reshape(slab_z, group_count, z_columns)
    result = jnp.einsum(
        "ij,jgk->igk",
        dz_full,
        lax.all_to_all(visc_panels, "grp", split_axis=1, concat_axis=0, tiled=True),
        precision=lax.Precision.HIGHEST,
    )
    dz_visc = lax.all_to_all(result, "grp", split_axis=0, concat_axis=1, tiled=True).reshape(
        slab_z, slab_y, cells_x
    )

    def to_lines(field):
        count = field.shape[0]
        return jnp.transpose(field, (0, 2, 1, 3)).reshape(count, slab_y, wide_count, y_columns)

    def from_lines(field):
        count = field.shape[0]
        return jnp.transpose(field.reshape(count, slab_y, slab_z, cells_x), (0, 2, 1, 3))

    def yline(block):
        return jnp.einsum("ij,cjgk->cigk", dy_full, block, precision=lax.Precision.HIGHEST)

    def y_derivative(field):
        lines = lax.all_to_all(to_lines(field), "wide", split_axis=2, concat_axis=1, tiled=True)
        return from_lines(
            lax.all_to_all(yline(lines), "wide", split_axis=1, concat_axis=2, tiled=True)
        )

    grad_x = along_last(velocity, dx_t)
    grad_y = y_derivative(velocity)
    s_xx = 2.0 * viscosity * grad_x[0]
    s_xy = viscosity * (grad_y[0] + grad_x[1])
    s_yy = 2.0 * viscosity * grad_y[1]
    s_xz = viscosity * grad_x[2]
    s_yz = viscosity * grad_y[2]
    dy_stress = y_derivative(jnp.stack([s_xy, s_yy, s_yz]))
    dx_stress = along_last(jnp.stack([s_xx, s_xy, s_xz]), dx_t)
    first = (dx_stress[0] + dy_stress[0] + dz_visc * grad_x[2]) / density
    second = (dx_stress[1] + dy_stress[1] + dz_visc * grad_y[2]) / density
    third = (dx_stress[2] + dy_stress[2]) / density
    return jnp.stack([first, second, third])


def shards(velocity, level_set):
    slab_z, slab_y, cells_x = level_set.shape
    count, group_count = lax.axis_size("wide"), lax.axis_size("grp")
    pairs = count > 1 and group_count > 1 and count & (count - 1) == 0 == group_count & (group_count - 1)
    if pairs and slab_z % count == 0 == cells_x % (128 * group_count) and slab_y % 16 == 0:
        return by_planes(velocity, level_set)
    return by_lines(velocity, level_set)


def solution(mesh):
    return jax.shard_map(
        shards,
        mesh=mesh,
        in_specs=(P(None, "grp", "wide", None), P("grp", "wide", None)),
        out_specs=P(None, "grp", "wide", None),
        check_vma=False,
    )
```

```python
import functools

import jax
import jax.numpy as jnp
import numpy as np
from jax import lax
from jax.experimental import pallas as pl
from jax.experimental.pallas import tpu as pltpu
from jax.sharding import PartitionSpec as P

interface_width = 1.0
flight = 5
mebibyte = 1024 * 1024
no_cost = pl.CostEstimate(flops=0, transcendentals=0, bytes_accessed=0)
small_cost = pl.CostEstimate(flops=10_000_000, transcendentals=0, bytes_accessed=0)


def derivative_table(count):
    offsets = np.arange(count)
    offset_mod = (offsets[:, None] - offsets[None, :]) % count
    angle_arg = np.pi * offset_mod / count
    safe_angle = np.where(offset_mod == 0, 0.5, angle_arg)
    parity = np.where(offset_mod % 2 == 0, 1.0, -1.0)
    entries = np.pi / count * parity * np.cos(safe_angle) / np.sin(safe_angle)
    return np.where(offset_mod == 0, 0.0, entries).astype(np.float32)


def halves(table):
    high = table.astype(jnp.bfloat16)
    low = (table - high.astype(np.float32)).astype(jnp.bfloat16)
    return high, low


def along_last(source, table_t):
    return jnp.dot(source, table_t, precision=lax.Precision.HIGHEST)


def properties(level_set):
    heavy = 0.5 * (1.0 + jnp.tanh(level_set / interface_width))
    return (0.2 + 0.8 * heavy, 0.25 + 0.75 * heavy)


def in_hbm(*arrays):
    return [pltpu.with_memory_space_constraint(x, pltpu.HBM) for x in arrays]


def pack_kernel(steps, planes, velocity, level_set, *refs):
    outs, sems = refs[-1 - len(steps) : -1], refs[-1]
    me = lax.axis_index("wide")
    copies = []
    for i, (out, (chunk, step)) in enumerate(zip(outs, steps)):
        plane = (me ^ step) * planes + chunk
        copies += [
            pltpu.make_async_copy(velocity.at[:, plane], out.at[0:3], sems.at[i, 0]),
            pltpu.make_async_copy(level_set.at[plane], out.at[3], sems.at[i, 1]),
        ]
    for copy in copies:
        copy.start()
    for copy in copies:
        copy.wait()


def pack(velocity, level_set, steps, planes, after=()):
    rows, cells = level_set.shape[1:]
    whole = pl.BlockSpec(memory_space=pl.ANY)
    hbm = pl.BlockSpec(memory_space=pltpu.HBM)
    return pl.pallas_call(
        functools.partial(pack_kernel, steps, planes),
        out_shape=(jax.ShapeDtypeStruct((4, rows, cells), jnp.float32),) * len(steps),
        in_specs=[hbm] * 2 + [whole] * len(after),
        out_specs=(pl.BlockSpec(memory_space=pltpu.VMEM),) * len(steps),
        scratch_shapes=[pltpu.SemaphoreType.DMA((len(steps), 2))],
        compiler_params=pltpu.CompilerParams(vmem_limit_bytes=4 * mebibyte),
        cost_estimate=no_cost,
        name="pack",
    )(*in_hbm(velocity, level_set), *after)


def split(value):
    high = value.astype(jnp.bfloat16)
    low = (value - high.astype(jnp.float32)).astype(jnp.bfloat16)
    return high, low


def times_x(fields, table):
    high, low = split(fields)
    return jnp.dot(
        jnp.concatenate([high, low, high], axis=1), table, preferred_element_type=jnp.float32
    )


def times_y(table, fields):
    high, low = split(fields)
    return jnp.dot(
        table, jnp.concatenate([high, high, low], axis=0), preferred_element_type=jnp.float32
    )


def plane_kernel(count, dx, dy, *refs):
    pieces, outs = refs[:count], refs[count : 2 * count]
    held, result = refs[2 * count :]
    me = lax.axis_index("wide")
    rows, cells = pieces[0].shape[1:]
    lines = rows * count
    for step in range(count):
        held[:, pl.ds(pl.multiple_of((me ^ step) * rows, 8), rows), :] = pieces[step][...]
    heavy = 0.5 * (1.0 + jnp.tanh(held[3] / interface_width))
    viscosity = 0.2 + 0.8 * heavy
    grad_x = times_x(held[0:3].reshape(3 * lines, cells), dx[...]).reshape(3, lines, cells)
    grad_y = times_y(dy[...], jnp.concatenate([held[0], held[1], held[2]], axis=1))
    grad_yu, grad_yv, grad_yw = (grad_y[:, i * cells : (i + 1) * cells] for i in range(3))
    s_xx = 2.0 * viscosity * grad_x[0]
    s_xy = viscosity * (grad_yu + grad_x[1])
    s_xz = viscosity * grad_x[2]
    s_yy = 2.0 * viscosity * grad_yv
    s_yz = viscosity * grad_yw
    along_x = times_x(jnp.concatenate([s_xx, s_xy, s_xz], axis=0), dx[...])
    along_y = times_y(dy[...], jnp.concatenate([s_xy, s_yy, s_yz], axis=1))
    for i in range(3):
        result[i] = (
            along_x[i * lines : (i + 1) * lines] + along_y[:, i * cells : (i + 1) * cells]
        )
    result[3] = grad_yw
    for step in range(count):
        outs[step][...] = result[:, pl.ds(pl.multiple_of((me ^ step) * rows, 8), rows), :]


def on_plane(pieces, dx, dy):
    count = len(pieces)
    rows, cells = pieces[0].shape[1:]
    vmem = pl.BlockSpec(memory_space=pltpu.VMEM)
    return pl.pallas_call(
        functools.partial(plane_kernel, count),
        out_shape=(jax.ShapeDtypeStruct((4, rows, cells), jnp.float32),) * count,
        in_specs=[vmem] * (2 + count),
        out_specs=(vmem,) * count,
        scratch_shapes=[pltpu.VMEM((4, rows * count, cells), jnp.float32)] * 2,
        compiler_params=pltpu.CompilerParams(vmem_limit_bytes=16 * mebibyte),
        cost_estimate=no_cost,
        name="plane",
    )(dx, dy, *pieces)


def join_kernel(steps, planes, *refs):
    pieces = refs[: len(steps)]
    inverse, first_add, cross = refs[len(steps) : len(steps) + 3]
    out, held, sems = refs[-3:]
    me = lax.axis_index("wide")
    copies = []
    for i, (chunk, step) in enumerate(steps):
        plane = (me ^ step) * planes + chunk
        piece = pieces[i]
        scale = inverse[plane]
        held[i, 0] = piece[0] * scale + first_add[plane]
        held[i, 1] = piece[1] * scale + piece[3] * cross[plane]
        held[i, 2] = piece[2] * scale
        copies.append(pltpu.make_async_copy(held.at[i], out.at[:, plane], sems.at[i]))
        copies[-1].start()
    for copy in copies:
        copy.wait()


def join(steps, pieces, fields, planes, total=None):
    shape = fields[0].shape
    vmem = pl.BlockSpec(memory_space=pltpu.VMEM)
    whole = pl.BlockSpec(memory_space=pl.ANY)
    extra = [] if total is None else [total]
    return pl.pallas_call(
        functools.partial(join_kernel, steps, planes),
        out_shape=jax.ShapeDtypeStruct((3,) + shape, jnp.float32),
        in_specs=[vmem] * (len(steps) + 3) + [whole] * len(extra),
        out_specs=whole,
        input_output_aliases={len(steps) + 3: 0} if extra else {},
        scratch_shapes=[
            pltpu.VMEM((len(steps), 3) + shape[1:], jnp.float32),
            pltpu.SemaphoreType.DMA((len(steps),)),
        ],
        compiler_params=pltpu.CompilerParams(vmem_limit_bytes=8 * mebibyte),
        cost_estimate=small_cost,
        name="join",
    )(*pieces, *fields, *extra)


def panel_kernel(count, level_set, after, *refs):
    outs, (held, sem) = refs[:count], refs[count:]
    copy = pltpu.make_async_copy(level_set, held, sem)
    copy.start()
    copy.wait()
    heavy = 0.5 * (1.0 + jnp.tanh(held[...] / interface_width))
    held[...] = 0.2 + 0.8 * heavy
    me = lax.axis_index("grp")
    width = outs[0].shape[2]
    for step in range(count):
        outs[step][...] = held[:, :, pl.ds(pl.multiple_of((me ^ step) * width, 128), width)]


def panels(level_set, after, count):
    slab, rows, cells = level_set.shape
    vmem = pl.BlockSpec(memory_space=pltpu.VMEM)
    return pl.pallas_call(
        functools.partial(panel_kernel, count),
        out_shape=(jax.ShapeDtypeStruct((slab, rows, cells // count), jnp.float32),) * count,
        in_specs=[pl.BlockSpec(memory_space=pltpu.HBM), pl.BlockSpec(memory_space=pl.ANY)],
        out_specs=(vmem,) * count,
        scratch_shapes=[pltpu.VMEM((slab, rows, cells), jnp.float32), pltpu.SemaphoreType.DMA],
        compiler_params=pltpu.CompilerParams(vmem_limit_bytes=6 * mebibyte),
        cost_estimate=no_cost,
        name="panels",
    )(*in_hbm(level_set), after)


def z_lines_kernel(count, tables, *refs):
    parts, outs, held = refs[:count], refs[count : 2 * count], refs[-1]
    slab, rows, _ = parts[0].shape
    for step in range(count):
        held[step * slab : (step + 1) * slab] = parts[step][...]
    table = tables[lax.axis_index("grp")]
    for row in range(rows):
        line = jnp.dot(
            table,
            held[:, row, :],
            precision=lax.Precision.HIGHEST,
            preferred_element_type=jnp.float32,
        )
        for step in range(count):
            outs[step][:, row, :] = line[step * slab : (step + 1) * slab]


def z_lines(tables, parts):
    count = len(parts)
    slab, rows, width = parts[0].shape
    vmem = pl.BlockSpec(memory_space=pltpu.VMEM)
    return pl.pallas_call(
        functools.partial(z_lines_kernel, count),
        out_shape=(jax.ShapeDtypeStruct(parts[0].shape, jnp.float32),) * count,
        in_specs=[vmem] * (1 + count),
        out_specs=(vmem,) * count,
        scratch_shapes=[pltpu.VMEM((slab * count, rows, width), jnp.float32)],
        compiler_params=pltpu.CompilerParams(vmem_limit_bytes=6 * mebibyte),
        cost_estimate=no_cost,
        name="z_lines",
    )(tables, *parts)


def prepare_kernel(count, dx, level_set, velocity, *refs):
    parts, (inverse, first_add, cross) = refs[:count], refs[count : count + 3]
    held, sems = refs[count + 3 :]
    copies = [
        pltpu.make_async_copy(level_set, held.at[0], sems.at[0]),
        pltpu.make_async_copy(velocity.at[2], held.at[1], sems.at[1]),
    ]
    for copy in copies:
        copy.start()
    for copy in copies:
        copy.wait()
    me = lax.axis_index("grp")
    width = parts[0].shape[2]
    slab, rows, cells = level_set.shape
    heavy = 0.5 * (1.0 + jnp.tanh(held[0] / interface_width))
    inverse[...] = 1.0 / (0.25 + 0.75 * heavy)
    for step in range(count):
        here = pl.ds(pl.multiple_of((me ^ step) * width, 128), width)
        cross[:, :, here] = parts[step][...] * inverse[:, :, here]
    grad = times_x(held[1].reshape(slab * rows, cells), dx[...]).reshape(slab, rows, cells)
    first_add[...] = cross[...] * grad


def prepare(dx, level_set, velocity, parts):
    vmem = pl.BlockSpec(memory_space=pltpu.VMEM)
    whole = pl.BlockSpec(memory_space=pltpu.HBM)
    return pl.pallas_call(
        functools.partial(prepare_kernel, len(parts)),
        out_shape=(jax.ShapeDtypeStruct(level_set.shape, jnp.float32),) * 3,
        in_specs=[vmem, whole, whole] + [vmem] * len(parts),
        out_specs=(vmem,) * 3,
        scratch_shapes=[
            pltpu.VMEM((2,) + level_set.shape, jnp.float32),
            pltpu.SemaphoreType.DMA((2,)),
        ],
        compiler_params=pltpu.CompilerParams(vmem_limit_bytes=16 * mebibyte),
        cost_estimate=no_cost,
        name="prepare",
    )(dx, *in_hbm(level_set, velocity), *parts)


def gate_kernel(*refs):
    pass


def gate(pieces, token, after):
    arrays = [*pieces, token]
    whole = pl.BlockSpec(memory_space=pl.ANY)
    outs = pl.pallas_call(
        gate_kernel,
        out_shape=tuple(jax.ShapeDtypeStruct(x.shape, x.dtype) for x in arrays),
        in_specs=[whole] * (len(arrays) + len(after)),
        out_specs=(whole,) * len(arrays),
        input_output_aliases={i: i for i in range(len(arrays))},
        compiler_params=pltpu.CompilerParams(vmem_limit_bytes=mebibyte),
        cost_estimate=small_cost,
        name="gate",
    )(*arrays, *after)
    return outs[:-1], outs[-1]


class Line:
    def __init__(self):
        self.arrived = []
        self.token = jnp.zeros((8, 128), jnp.float32)

    def send(self, piece, axis, step, after=()):
        count = lax.axis_size(axis)
        if len(self.arrived) >= flight:
            (piece,), self.token = gate([piece], self.token, [self.arrived[-flight], *after])
        got = lax.ppermute(piece, axis, [(i, i ^ step) for i in range(count)])
        self.arrived.append(got)
        return got


def turns(first, second):
    both = [x for pair in zip(first, second) for x in pair]
    shorter = min(len(first), len(second))
    return both + list(first[shorter:]) + list(second[shorter:])


def message_order(count, planes, group_count):
    far, near = range(count // 2, count), range(1, count // 2)
    out = [("out", chunk, step) for chunk in range(planes) for step in turns(far, near)]
    back = [("back", chunk, step) for chunk in range(planes - 1) for step in turns(far, near)]
    back += [("back", planes - 1, step) for step in turns(near, far)]
    first_z = count - 1
    second_z = max(len(out) + 3, first_z + 2 * (group_count - 2) + 1)
    order = []
    for place, message in enumerate(out + back + [None] * 2 * (second_z + 2 * group_count)):
        for start, kind in ((first_z, "z_out"), (second_z, "z_back")):
            step, odd = divmod(place - start, 2)
            if not odd and 0 <= step < group_count - 1:
                order.append((kind, 0, step + 1))
        if message is not None:
            order.append(message)
    return order


def by_planes(velocity, level_set):
    cells_x = velocity.shape[3]
    slab_z, slab_y = velocity.shape[1:3]
    count = lax.axis_size("wide")
    group_count = lax.axis_size("grp")
    planes = slab_z // count
    high, low = halves(derivative_table(cells_x).T)
    dx = jnp.asarray(np.concatenate([high, high, low], axis=0))
    high, low = halves(derivative_table(slab_y * count))
    dy = jnp.asarray(np.concatenate([high, low, high], axis=1))
    table_z = derivative_table(slab_z * group_count)
    table_z = table_z.reshape(group_count, slab_z, group_count, slab_z)
    partners = [place ^ np.arange(group_count) for place in range(group_count)]
    tables = jnp.asarray(
        np.stack([table_z[p][:, :, p].reshape((slab_z * group_count,) * 2) for p in partners])
    )

    order = message_order(count, planes, group_count)
    leaving = [(chunk, step) for kind, chunk, step in order if kind == "out"]
    own = [(chunk, 0) for chunk in range(planes)]
    sent, packed = {}, []
    for steps in (leaving[:1], own + leaving[1:flight], leaving[flight:]):
        if not steps:
            continue
        packed = pack(velocity, level_set, steps, planes, packed)
        sent.update(zip(steps, packed))

    line = Line()
    arrived = {place: sent[place] for place in own}
    result, returned = {}, {}
    panel, z_arrived, z_result, z_returned = None, {}, None, {}

    def plane(chunk):
        if chunk not in result:
            result[chunk] = on_plane([arrived[chunk, i] for i in range(count)], dx, dy)
            returned[chunk, 0] = result[chunk][0]

    for place, (kind, chunk, step) in enumerate(order):
        after = ()
        if place + flight < len(order):
            ahead, coming, _ = order[place + flight]
            known = all((coming, i) in arrived for i in range(count))
            if ahead == "back" and coming > 0 and coming not in result and known:
                plane(coming)
                after = result[coming][:1]
        if kind == "out":
            arrived[chunk, step] = line.send(sent[chunk, step], "wide", step, after)
        elif kind == "back":
            plane(chunk)
            returned[chunk, step] = line.send(result[chunk][step], "wide", step, after)
        elif kind == "z_out":
            if panel is None:
                panel = panels(level_set, line.arrived[0], group_count)
                z_arrived[0] = panel[0]
            z_arrived[step] = line.send(panel[step], "grp", step, after)
        else:
            if z_result is None:
                z_result = z_lines(tables, [z_arrived[i] for i in range(group_count)])
                z_returned[0] = z_result[0]
            z_returned[step] = line.send(z_result[step], "grp", step, after)

    fields = prepare(dx, level_set, velocity, [z_returned[i] for i in range(group_count)])
    total = None
    early = [(c, i) for c in range(planes - 1) for i in range(count)] + [(planes - 1, 0)]
    late = [(c, step) for kind, c, step in order if kind == "back" and c == planes - 1]
    for steps in [early] + [[piece] for piece in late[:-3]] + [late[-3:]]:
        total = join(steps, [returned[piece] for piece in steps], fields, planes, total)
    return total


def by_lines(velocity, level_set):
    cells_x = velocity.shape[3]
    slab_z = velocity.shape[1]
    slab_y = velocity.shape[2]
    wide_count = lax.axis_size("wide")
    group_count = lax.axis_size("grp")
    cells_y = slab_y * wide_count
    cells_z = slab_z * group_count
    dx_t = jnp.asarray(derivative_table(cells_x).T)
    dy_full = jnp.asarray(derivative_table(cells_y))
    dz_full = jnp.asarray(derivative_table(cells_z))
    viscosity, density = properties(level_set)
    z_columns = slab_y * cells_x // group_count
    y_columns = slab_z * cells_x // wide_count
    visc_panels = viscosity.reshape(slab_z, group_count, z_columns)
    result = jnp.einsum(
        "ij,jgk->igk",
        dz_full,
        lax.all_to_all(visc_panels, "grp", split_axis=1, concat_axis=0, tiled=True),
        precision=lax.Precision.HIGHEST,
    )
    dz_visc = lax.all_to_all(result, "grp", split_axis=0, concat_axis=1, tiled=True).reshape(
        slab_z, slab_y, cells_x
    )

    def to_lines(field):
        count = field.shape[0]
        return jnp.transpose(field, (0, 2, 1, 3)).reshape(count, slab_y, wide_count, y_columns)

    def from_lines(field):
        count = field.shape[0]
        return jnp.transpose(field.reshape(count, slab_y, slab_z, cells_x), (0, 2, 1, 3))

    def yline(block):
        return jnp.einsum("ij,cjgk->cigk", dy_full, block, precision=lax.Precision.HIGHEST)

    def y_derivative(field):
        lines = lax.all_to_all(to_lines(field), "wide", split_axis=2, concat_axis=1, tiled=True)
        return from_lines(
            lax.all_to_all(yline(lines), "wide", split_axis=1, concat_axis=2, tiled=True)
        )

    grad_x = along_last(velocity, dx_t)
    grad_y = y_derivative(velocity)
    s_xx = 2.0 * viscosity * grad_x[0]
    s_xy = viscosity * (grad_y[0] + grad_x[1])
    s_yy = 2.0 * viscosity * grad_y[1]
    s_xz = viscosity * grad_x[2]
    s_yz = viscosity * grad_y[2]
    dy_stress = y_derivative(jnp.stack([s_xy, s_yy, s_yz]))
    dx_stress = along_last(jnp.stack([s_xx, s_xy, s_xz]), dx_t)
    first = (dx_stress[0] + dy_stress[0] + dz_visc * grad_x[2]) / density
    second = (dx_stress[1] + dy_stress[1] + dz_visc * grad_y[2]) / density
    third = (dx_stress[2] + dy_stress[2]) / density
    return jnp.stack([first, second, third])


def shards(velocity, level_set):
    slab_z, slab_y, cells_x = level_set.shape
    count, group_count = lax.axis_size("wide"), lax.axis_size("grp")
    pairs = count > 1 and group_count > 1 and count & (count - 1) == 0 == group_count & (group_count - 1)
    if pairs and slab_z % count == 0 == cells_x % (128 * group_count) and slab_y % 16 == 0:
        return by_planes(velocity, level_set)
    return by_lines(velocity, level_set)


def solution(mesh):
    return jax.shard_map(
        shards,
        mesh=mesh,
        in_specs=(P(None, "grp", "wide", None), P("grp", "wide", None)),
        out_specs=P(None, "grp", "wide", None),
        check_vma=False,
    )
```

```python
import functools

import jax
import jax.numpy as jnp
import numpy as np
from jax import lax
from jax.experimental import pallas as pl
from jax.experimental.pallas import tpu as pltpu
from jax.sharding import PartitionSpec as P

interface_width = 1.0
flight = 5
mebibyte = 1024 * 1024
no_cost = pl.CostEstimate(flops=0, transcendentals=0, bytes_accessed=0)
small_cost = pl.CostEstimate(flops=10_000_000, transcendentals=0, bytes_accessed=0)


def derivative_table(count):
    offsets = np.arange(count)
    offset_mod = (offsets[:, None] - offsets[None, :]) % count
    angle_arg = np.pi * offset_mod / count
    safe_angle = np.where(offset_mod == 0, 0.5, angle_arg)
    parity = np.where(offset_mod % 2 == 0, 1.0, -1.0)
    entries = np.pi / count * parity * np.cos(safe_angle) / np.sin(safe_angle)
    return np.where(offset_mod == 0, 0.0, entries).astype(np.float32)


def halves(table):
    high = table.astype(jnp.bfloat16)
    low = (table - high.astype(np.float32)).astype(jnp.bfloat16)
    return high, low


def along_last(source, table_t):
    return jnp.dot(source, table_t, precision=lax.Precision.HIGHEST)


def properties(level_set):
    heavy = 0.5 * (1.0 + jnp.tanh(level_set / interface_width))
    return (0.2 + 0.8 * heavy, 0.25 + 0.75 * heavy)


def in_hbm(*arrays):
    return [pltpu.with_memory_space_constraint(x, pltpu.HBM) for x in arrays]


def pack_kernel(steps, planes, velocity, level_set, *refs):
    outs, sems = refs[-1 - len(steps) : -1], refs[-1]
    me = lax.axis_index("wide")
    copies = []
    for i, (out, (chunk, step)) in enumerate(zip(outs, steps)):
        plane = (me ^ step) * planes + chunk
        copies += [
            pltpu.make_async_copy(velocity.at[:, plane], out.at[0:3], sems.at[i, 0]),
            pltpu.make_async_copy(level_set.at[plane], out.at[3], sems.at[i, 1]),
        ]
    for copy in copies:
        copy.start()
    for copy in copies:
        copy.wait()


def pack(velocity, level_set, steps, planes, after=()):
    rows, cells = level_set.shape[1:]
    whole = pl.BlockSpec(memory_space=pl.ANY)
    hbm = pl.BlockSpec(memory_space=pltpu.HBM)
    return pl.pallas_call(
        functools.partial(pack_kernel, steps, planes),
        out_shape=(jax.ShapeDtypeStruct((4, rows, cells), jnp.float32),) * len(steps),
        in_specs=[hbm] * 2 + [whole] * len(after),
        out_specs=(pl.BlockSpec(memory_space=pltpu.VMEM),) * len(steps),
        scratch_shapes=[pltpu.SemaphoreType.DMA((len(steps), 2))],
        compiler_params=pltpu.CompilerParams(vmem_limit_bytes=4 * mebibyte),
        cost_estimate=no_cost,
        name="pack",
    )(*in_hbm(velocity, level_set), *after)


def split(value):
    high = value.astype(jnp.bfloat16)
    low = (value - high.astype(jnp.float32)).astype(jnp.bfloat16)
    return high, low


def times_x(fields, table):
    high, low = split(fields)
    return jnp.dot(
        jnp.concatenate([high, low, high], axis=1), table, preferred_element_type=jnp.float32
    )


def times_y(table, fields):
    high, low = split(fields)
    return jnp.dot(
        table, jnp.concatenate([high, high, low], axis=0), preferred_element_type=jnp.float32
    )


def plane_kernel(count, dx, dy, *refs):
    pieces, outs = refs[:count], refs[count : 2 * count]
    held, result = refs[2 * count :]
    me = lax.axis_index("wide")
    rows, cells = pieces[0].shape[1:]
    lines = rows * count
    for step in range(count):
        held[:, pl.ds(pl.multiple_of((me ^ step) * rows, 8), rows), :] = pieces[step][...]
    heavy = 0.5 * (1.0 + jnp.tanh(held[3] / interface_width))
    viscosity = 0.2 + 0.8 * heavy
    grad_x = times_x(held[0:3].reshape(3 * lines, cells), dx[...]).reshape(3, lines, cells)
    grad_y = times_y(dy[...], jnp.concatenate([held[0], held[1], held[2]], axis=1))
    grad_yu, grad_yv, grad_yw = (grad_y[:, i * cells : (i + 1) * cells] for i in range(3))
    s_xx = 2.0 * viscosity * grad_x[0]
    s_xy = viscosity * (grad_yu + grad_x[1])
    s_xz = viscosity * grad_x[2]
    s_yy = 2.0 * viscosity * grad_yv
    s_yz = viscosity * grad_yw
    along_x = times_x(jnp.concatenate([s_xx, s_xy, s_xz], axis=0), dx[...])
    along_y = times_y(dy[...], jnp.concatenate([s_xy, s_yy, s_yz], axis=1))
    for i in range(3):
        result[i] = (
            along_x[i * lines : (i + 1) * lines] + along_y[:, i * cells : (i + 1) * cells]
        )
    result[3] = grad_yw
    for step in range(count):
        outs[step][...] = result[:, pl.ds(pl.multiple_of((me ^ step) * rows, 8), rows), :]


def on_plane(pieces, dx, dy):
    count = len(pieces)
    rows, cells = pieces[0].shape[1:]
    vmem = pl.BlockSpec(memory_space=pltpu.VMEM)
    return pl.pallas_call(
        functools.partial(plane_kernel, count),
        out_shape=(jax.ShapeDtypeStruct((4, rows, cells), jnp.float32),) * count,
        in_specs=[vmem] * (2 + count),
        out_specs=(vmem,) * count,
        scratch_shapes=[pltpu.VMEM((4, rows * count, cells), jnp.float32)] * 2,
        compiler_params=pltpu.CompilerParams(vmem_limit_bytes=16 * mebibyte),
        cost_estimate=no_cost,
        name="plane",
    )(dx, dy, *pieces)


def join_kernel(steps, planes, *refs):
    pieces = refs[: len(steps)]
    inverse, first_add, cross = refs[len(steps) : len(steps) + 3]
    out, held, sems = refs[-3:]
    me = lax.axis_index("wide")
    copies = []
    for i, (chunk, step) in enumerate(steps):
        plane = (me ^ step) * planes + chunk
        piece = pieces[i]
        scale = inverse[plane]
        held[i, 0] = piece[0] * scale + first_add[plane]
        held[i, 1] = piece[1] * scale + piece[3] * cross[plane]
        held[i, 2] = piece[2] * scale
        copies.append(pltpu.make_async_copy(held.at[i], out.at[:, plane], sems.at[i]))
        copies[-1].start()
    for copy in copies:
        copy.wait()


def join(steps, pieces, fields, planes, total=None):
    shape = fields[0].shape
    vmem = pl.BlockSpec(memory_space=pltpu.VMEM)
    whole = pl.BlockSpec(memory_space=pl.ANY)
    extra = [] if total is None else [total]
    return pl.pallas_call(
        functools.partial(join_kernel, steps, planes),
        out_shape=jax.ShapeDtypeStruct((3,) + shape, jnp.float32),
        in_specs=[vmem] * (len(steps) + 3) + [whole] * len(extra),
        out_specs=whole,
        input_output_aliases={len(steps) + 3: 0} if extra else {},
        scratch_shapes=[
            pltpu.VMEM((len(steps), 3) + shape[1:], jnp.float32),
            pltpu.SemaphoreType.DMA((len(steps),)),
        ],
        compiler_params=pltpu.CompilerParams(vmem_limit_bytes=8 * mebibyte),
        cost_estimate=small_cost,
        name="join",
    )(*pieces, *fields, *extra)


def panel_kernel(count, level_set, after, *refs):
    outs, (held, sem) = refs[:count], refs[count:]
    copy = pltpu.make_async_copy(level_set, held, sem)
    copy.start()
    copy.wait()
    heavy = 0.5 * (1.0 + jnp.tanh(held[...] / interface_width))
    held[...] = 0.2 + 0.8 * heavy
    me = lax.axis_index("grp")
    width = outs[0].shape[2]
    for step in range(count):
        outs[step][...] = held[:, :, pl.ds(pl.multiple_of((me ^ step) * width, 128), width)]


def panels(level_set, after, count):
    slab, rows, cells = level_set.shape
    vmem = pl.BlockSpec(memory_space=pltpu.VMEM)
    return pl.pallas_call(
        functools.partial(panel_kernel, count),
        out_shape=(jax.ShapeDtypeStruct((slab, rows, cells // count), jnp.float32),) * count,
        in_specs=[pl.BlockSpec(memory_space=pltpu.HBM), pl.BlockSpec(memory_space=pl.ANY)],
        out_specs=(vmem,) * count,
        scratch_shapes=[pltpu.VMEM((slab, rows, cells), jnp.float32), pltpu.SemaphoreType.DMA],
        compiler_params=pltpu.CompilerParams(vmem_limit_bytes=6 * mebibyte),
        cost_estimate=no_cost,
        name="panels",
    )(*in_hbm(level_set), after)


def z_lines_kernel(count, tables, *refs):
    parts, outs, held = refs[:count], refs[count : 2 * count], refs[-1]
    slab, rows, _ = parts[0].shape
    for step in range(count):
        held[step * slab : (step + 1) * slab] = parts[step][...]
    table = tables[lax.axis_index("grp")]
    for row in range(rows):
        line = jnp.dot(
            table,
            held[:, row, :],
            precision=lax.Precision.HIGHEST,
            preferred_element_type=jnp.float32,
        )
        for step in range(count):
            outs[step][:, row, :] = line[step * slab : (step + 1) * slab]


def z_lines(tables, parts):
    count = len(parts)
    slab, rows, width = parts[0].shape
    vmem = pl.BlockSpec(memory_space=pltpu.VMEM)
    return pl.pallas_call(
        functools.partial(z_lines_kernel, count),
        out_shape=(jax.ShapeDtypeStruct(parts[0].shape, jnp.float32),) * count,
        in_specs=[vmem] * (1 + count),
        out_specs=(vmem,) * count,
        scratch_shapes=[pltpu.VMEM((slab * count, rows, width), jnp.float32)],
        compiler_params=pltpu.CompilerParams(vmem_limit_bytes=6 * mebibyte),
        cost_estimate=no_cost,
        name="z_lines",
    )(tables, *parts)


def prepare_kernel(count, dx, level_set, velocity, *refs):
    parts, (inverse, first_add, cross) = refs[:count], refs[count : count + 3]
    held, sems = refs[count + 3 :]
    copies = [
        pltpu.make_async_copy(level_set, held.at[0], sems.at[0]),
        pltpu.make_async_copy(velocity.at[2], held.at[1], sems.at[1]),
    ]
    for copy in copies:
        copy.start()
    for copy in copies:
        copy.wait()
    me = lax.axis_index("grp")
    width = parts[0].shape[2]
    slab, rows, cells = level_set.shape
    heavy = 0.5 * (1.0 + jnp.tanh(held[0] / interface_width))
    inverse[...] = 1.0 / (0.25 + 0.75 * heavy)
    for step in range(count):
        here = pl.ds(pl.multiple_of((me ^ step) * width, 128), width)
        cross[:, :, here] = parts[step][...] * inverse[:, :, here]
    grad = times_x(held[1].reshape(slab * rows, cells), dx[...]).reshape(slab, rows, cells)
    first_add[...] = cross[...] * grad


def prepare(dx, level_set, velocity, parts):
    vmem = pl.BlockSpec(memory_space=pltpu.VMEM)
    whole = pl.BlockSpec(memory_space=pltpu.HBM)
    return pl.pallas_call(
        functools.partial(prepare_kernel, len(parts)),
        out_shape=(jax.ShapeDtypeStruct(level_set.shape, jnp.float32),) * 3,
        in_specs=[vmem, whole, whole] + [vmem] * len(parts),
        out_specs=(vmem,) * 3,
        scratch_shapes=[
            pltpu.VMEM((2,) + level_set.shape, jnp.float32),
            pltpu.SemaphoreType.DMA((2,)),
        ],
        compiler_params=pltpu.CompilerParams(vmem_limit_bytes=16 * mebibyte),
        cost_estimate=no_cost,
        name="prepare",
    )(dx, *in_hbm(level_set, velocity), *parts)


def gate_kernel(*refs):
    pass


def gate(pieces, token, after):
    arrays = [*pieces, token]
    whole = pl.BlockSpec(memory_space=pl.ANY)
    outs = pl.pallas_call(
        gate_kernel,
        out_shape=tuple(jax.ShapeDtypeStruct(x.shape, x.dtype) for x in arrays),
        in_specs=[whole] * (len(arrays) + len(after)),
        out_specs=(whole,) * len(arrays),
        input_output_aliases={i: i for i in range(len(arrays))},
        compiler_params=pltpu.CompilerParams(vmem_limit_bytes=mebibyte),
        cost_estimate=small_cost,
        name="gate",
    )(*arrays, *after)
    return outs[:-1], outs[-1]


class Line:
    def __init__(self):
        self.arrived = []
        self.token = jnp.zeros((8, 128), jnp.float32)

    def send(self, piece, axis, step, after=()):
        count = lax.axis_size(axis)
        if len(self.arrived) >= flight:
            (piece,), self.token = gate([piece], self.token, [self.arrived[-flight], *after])
        got = lax.ppermute(piece, axis, [(i, i ^ step) for i in range(count)])
        self.arrived.append(got)
        return got


def turns(first, second):
    both = [x for pair in zip(first, second) for x in pair]
    shorter = min(len(first), len(second))
    return both + list(first[shorter:]) + list(second[shorter:])


measured_steps = {
    (8, 2): (
        (6, 1, 4, 3, 5, 2, 7),
        (4, 1, 5, 2, 6, 3, 7),
        (6, 3, 5, 2, 4, 1, 7),
        (1, 4, 3, 5, 2, 6, 7),
    )
}


def message_order(count, planes, group_count):
    far, near = range(count // 2, count), range(1, count // 2)
    phases = [turns(far, near)] * (2 * planes - 1) + [turns(near, far)]
    phases = measured_steps.get((count, planes), phases)
    out = [("out", chunk, step) for chunk in range(planes) for step in phases[chunk]]
    back = [("back", chunk, step) for chunk in range(planes) for step in phases[planes + chunk]]
    first_z = count - 1
    second_z = max(len(out) + 3, first_z + 2 * (group_count - 2) + 1)
    order = []
    for place, message in enumerate(out + back + [None] * 2 * (second_z + 2 * group_count)):
        for start, kind in ((first_z, "z_out"), (second_z, "z_back")):
            step, odd = divmod(place - start, 2)
            if not odd and 0 <= step < group_count - 1:
                order.append((kind, 0, step + 1))
        if message is not None:
            order.append(message)
    return order


def by_planes(velocity, level_set):
    cells_x = velocity.shape[3]
    slab_z, slab_y = velocity.shape[1:3]
    count = lax.axis_size("wide")
    group_count = lax.axis_size("grp")
    planes = slab_z // count
    high, low = halves(derivative_table(cells_x).T)
    dx = jnp.asarray(np.concatenate([high, high, low], axis=0))
    high, low = halves(derivative_table(slab_y * count))
    dy = jnp.asarray(np.concatenate([high, low, high], axis=1))
    table_z = derivative_table(slab_z * group_count)
    table_z = table_z.reshape(group_count, slab_z, group_count, slab_z)
    partners = [place ^ np.arange(group_count) for place in range(group_count)]
    tables = jnp.asarray(
        np.stack([table_z[p][:, :, p].reshape((slab_z * group_count,) * 2) for p in partners])
    )

    order = message_order(count, planes, group_count)
    leaving = [(chunk, step) for kind, chunk, step in order if kind == "out"]
    own = [(chunk, 0) for chunk in range(planes)]
    sent, packed = {}, []
    for steps in (leaving[:1], own + leaving[1:flight], leaving[flight:]):
        if not steps:
            continue
        packed = pack(velocity, level_set, steps, planes, packed)
        sent.update(zip(steps, packed))

    line = Line()
    arrived = {place: sent[place] for place in own}
    result, returned = {}, {}
    panel, z_arrived, z_result, z_returned = None, {}, None, {}

    def plane(chunk):
        if chunk not in result:
            result[chunk] = on_plane([arrived[chunk, i] for i in range(count)], dx, dy)
            returned[chunk, 0] = result[chunk][0]

    for place, (kind, chunk, step) in enumerate(order):
        after = ()
        if place + flight < len(order):
            ahead, coming, _ = order[place + flight]
            known = all((coming, i) in arrived for i in range(count))
            if ahead == "back" and coming > 0 and coming not in result and known:
                plane(coming)
                after = result[coming][:1]
        if kind == "out":
            arrived[chunk, step] = line.send(sent[chunk, step], "wide", step, after)
        elif kind == "back":
            plane(chunk)
            returned[chunk, step] = line.send(result[chunk][step], "wide", step, after)
        elif kind == "z_out":
            if panel is None:
                panel = panels(level_set, line.arrived[0], group_count)
                z_arrived[0] = panel[0]
            z_arrived[step] = line.send(panel[step], "grp", step, after)
        else:
            if z_result is None:
                z_result = z_lines(tables, [z_arrived[i] for i in range(group_count)])
                z_returned[0] = z_result[0]
            z_returned[step] = line.send(z_result[step], "grp", step, after)

    fields = prepare(dx, level_set, velocity, [z_returned[i] for i in range(group_count)])
    total = None
    early = [(c, i) for c in range(planes - 1) for i in range(count)] + [(planes - 1, 0)]
    late = [(c, step) for kind, c, step in order if kind == "back" and c == planes - 1]
    for steps in [early] + [[piece] for piece in late[:-3]] + [late[-3:]]:
        total = join(steps, [returned[piece] for piece in steps], fields, planes, total)
    return total


def by_lines(velocity, level_set):
    cells_x = velocity.shape[3]
    slab_z = velocity.shape[1]
    slab_y = velocity.shape[2]
    wide_count = lax.axis_size("wide")
    group_count = lax.axis_size("grp")
    cells_y = slab_y * wide_count
    cells_z = slab_z * group_count
    dx_t = jnp.asarray(derivative_table(cells_x).T)
    dy_full = jnp.asarray(derivative_table(cells_y))
    dz_full = jnp.asarray(derivative_table(cells_z))
    viscosity, density = properties(level_set)
    z_columns = slab_y * cells_x // group_count
    y_columns = slab_z * cells_x // wide_count
    visc_panels = viscosity.reshape(slab_z, group_count, z_columns)
    result = jnp.einsum(
        "ij,jgk->igk",
        dz_full,
        lax.all_to_all(visc_panels, "grp", split_axis=1, concat_axis=0, tiled=True),
        precision=lax.Precision.HIGHEST,
    )
    dz_visc = lax.all_to_all(result, "grp", split_axis=0, concat_axis=1, tiled=True).reshape(
        slab_z, slab_y, cells_x
    )

    def to_lines(field):
        count = field.shape[0]
        return jnp.transpose(field, (0, 2, 1, 3)).reshape(count, slab_y, wide_count, y_columns)

    def from_lines(field):
        count = field.shape[0]
        return jnp.transpose(field.reshape(count, slab_y, slab_z, cells_x), (0, 2, 1, 3))

    def yline(block):
        return jnp.einsum("ij,cjgk->cigk", dy_full, block, precision=lax.Precision.HIGHEST)

    def y_derivative(field):
        lines = lax.all_to_all(to_lines(field), "wide", split_axis=2, concat_axis=1, tiled=True)
        return from_lines(
            lax.all_to_all(yline(lines), "wide", split_axis=1, concat_axis=2, tiled=True)
        )

    grad_x = along_last(velocity, dx_t)
    grad_y = y_derivative(velocity)
    s_xx = 2.0 * viscosity * grad_x[0]
    s_xy = viscosity * (grad_y[0] + grad_x[1])
    s_yy = 2.0 * viscosity * grad_y[1]
    s_xz = viscosity * grad_x[2]
    s_yz = viscosity * grad_y[2]
    dy_stress = y_derivative(jnp.stack([s_xy, s_yy, s_yz]))
    dx_stress = along_last(jnp.stack([s_xx, s_xy, s_xz]), dx_t)
    first = (dx_stress[0] + dy_stress[0] + dz_visc * grad_x[2]) / density
    second = (dx_stress[1] + dy_stress[1] + dz_visc * grad_y[2]) / density
    third = (dx_stress[2] + dy_stress[2]) / density
    return jnp.stack([first, second, third])


def shards(velocity, level_set):
    slab_z, slab_y, cells_x = level_set.shape
    count, group_count = lax.axis_size("wide"), lax.axis_size("grp")
    pairs = count > 1 and group_count > 1 and count & (count - 1) == 0 == group_count & (group_count - 1)
    if pairs and slab_z % count == 0 == cells_x % (128 * group_count) and slab_y % 16 == 0:
        return by_planes(velocity, level_set)
    return by_lines(velocity, level_set)


def solution(mesh):
    return jax.shard_map(
        shards,
        mesh=mesh,
        in_specs=(P(None, "grp", "wide", None), P("grp", "wide", None)),
        out_specs=P(None, "grp", "wide", None),
        check_vma=False,
    )
```
